256 devices in a mesh: grp: 16 (over x_lo, z), blk: 16 (over x_hi, y, core).
Axes of the slice: x: 4 (x_hi: 2, x_lo: 2; x = x_hi * 2 + x_lo), y: 4, z: 8, core: 2. Of those that a mesh axis runs over, the one named last changes fastest.
Arguments:
- source_vectors: float32 [196608, 768], P(('grp', 'blk')), may hold values from -1.2 to 1.2
- reference_vectors: float32 [8192, 768], P(('grp', 'blk')), may hold values from -1.2 to 1.2
- linked_target: int32 [196608], P(('grp', 'blk')), may hold values from 0 to 8191, as said below
- score_multiplier: float32 [1], replicated, may hold values from 1 to 3
- score_offset: float32 [1], replicated, may hold values from -3 to -1
Outputs:
- row_loss: float32 [196608], P(('grp', 'blk'))
- citing_grad: float32 [196608, 768], P(('grp', 'blk'))
- cited_grad: float32 [8192, 768], P(('grp', 'blk'))
The draws below stay inside these ranges and needn't reach their ends.
Inputs may be any that keep to these rules, and one draw needn't show every extreme that they name: `linked_target`: positive of a citing row is a cited row within that row's band.
All inputs are finite; a program needn't handle non-finite values.
Results may differ from the reference program's by a relative error of at most 0.0037.
Values may be sent and summed in bfloat16 or wider, within the bound.
No kernel may reach another device: no remote copies, remote signals or barrier semaphores. Data moves between devices by JAX's collectives and lax.ppermute only.
A program may use at most 64 MiB of HBM per device.

```python
import math
import jax
import jax.numpy as jnp
from jax import lax

D = 768
ROWS_DEV = 768
CITED_DEV = 32
STEPS = 8
PAIRS = 4096
ROWS = 196608
CITED = 8192
N_GRP = 16
N_BLK = 16
DEVICES = 256


def draw_linked_target(key, part):
    key = jax.random.fold_in(key, 7)
    first, second, third = jax.random.split(key, 3)
    device_ids = jnp.arange(ROWS, dtype=jnp.int32) // ROWS_DEV
    block_index = device_ids % N_BLK
    offsets = jax.random.randint(first, (ROWS,), 0, STEPS, dtype=jnp.int32) - (STEPS // 2 - 1)
    groups = jax.random.randint(second, (ROWS,), 0, N_GRP, dtype=jnp.int32)
    local_part = jax.random.randint(third, (ROWS,), 0, CITED_DEV, dtype=jnp.int32)
    column = (block_index + offsets) % N_BLK
    return ((groups * N_BLK + column) * CITED_DEV + local_part).astype(jnp.int32)


def steps_of(rng, extent, pieces, least, largest):
    loudness, own = 1.0, jax.random.fold_in(rng, 6)
    for dim, parts in pieces:
        heights = jnp.exp(jax.random.uniform(jax.random.fold_in(own, dim), (parts,), jnp.float32, least / len(pieces), largest / len(pieces)))
        loudness = loudness * jnp.repeat(heights, extent[dim] // parts).reshape([-1 if axis == dim else 1 for axis in range(len(extent))])
    return loudness


def centred(stream_key, extent, width, bound, pieces=(), kind=jnp.bfloat16):
    factor_of = steps_of(stream_key, extent, pieces, -0.22, 0.18) if pieces else 1.0
    drawn = jax.random.normal(stream_key, extent, jnp.float32) * width * factor_of
    return jnp.minimum(jnp.maximum(drawn, -bound), bound).astype(kind)


def setup_inputs(seed: int = 0) -> dict:
    splits = jax.random.split(jax.random.key(seed), 6)
    source_vectors = centred(splits[0], (ROWS, D), 0.19, 1.2, ((0, 256),), jnp.float32)
    reference_vectors = centred(splits[1], (CITED, D), 0.19, 1.2, ((0, 256),), jnp.float32)
    linked_target = draw_linked_target(jax.random.fold_in(splits[5], 71), 0)
    score_multiplier = jnp.clip(jax.random.uniform(splits[3], (1,), jnp.float32, 1.0, 3.0), 1.0, 3.0)
    score_offset = jnp.clip(jax.random.uniform(splits[4], (1,), jnp.float32, -3.0, -1.0), -3.0, -1.0)
    return dict(source_vectors=source_vectors, reference_vectors=reference_vectors, linked_target=linked_target, score_multiplier=score_multiplier, score_offset=score_offset)


def window_ids(block_index):
    groups = jnp.arange(N_GRP, dtype=jnp.int32)[:, None, None]
    offsets = jnp.arange(STEPS, dtype=jnp.int32)[None, :, None] - (STEPS // 2 - 1)
    local_part = jnp.arange(CITED_DEV, dtype=jnp.int32)[None, None, :]
    column = (block_index + offsets) % N_BLK
    return ((groups * N_BLK + column) * CITED_DEV + local_part).reshape(-1).astype(jnp.int32)

def reference(source_vectors, reference_vectors, linked_target, score_multiplier, score_offset):
    averaging_count = 1.0 / math.sqrt(PAIRS)
    couple_factor = score_multiplier[0] * averaging_count
    citing_half_precision = source_vectors.astype(jnp.bfloat16).reshape(DEVICES, ROWS_DEV, D)
    cited_bf = reference_vectors.astype(jnp.bfloat16)
    labels_all = linked_target.reshape(DEVICES, ROWS_DEV)
    devices = jnp.arange(DEVICES, dtype=jnp.int32)

    def per_block(total, inputs):
        device, source_entries, pos_rows = inputs
        ids = window_ids(device % N_BLK)
        referenced_span = cited_bf[ids]
        score_table = score_multiplier[0] * jnp.dot(source_entries, referenced_span.T, preferred_element_type=jnp.float32) + score_offset[0]
        label = ids[None, :] == pos_rows[:, None]
        loss = lax.optimization_barrier(jnp.sum(jax.nn.softplus(jnp.where(label, -score_table, score_table)), axis=1)) * averaging_count
        grad = ((jax.nn.sigmoid(score_table) - label.astype(jnp.float32)) * couple_factor).astype(jnp.bfloat16)
        citing_part = jnp.dot(grad, referenced_span, preferred_element_type=jnp.float32)
        cited_part = jnp.dot(grad.T, source_entries, preferred_element_type=jnp.float32)
        total = total.at[ids].add(cited_part)
        return (total, (loss, citing_part))
    start = jnp.zeros((CITED, D), jnp.float32)
    cited_grad, (row_loss, citing_grad) = lax.scan(per_block, start, (devices, citing_half_precision, labels_all))
    return (row_loss.reshape(ROWS), citing_grad.reshape(ROWS, D), cited_grad)
```

```python
import functools
import math

import jax
import jax.numpy as jnp
from jax import lax
from jax.experimental import pallas as pl
from jax.experimental.pallas import tpu as pltpu
from jax.sharding import PartitionSpec as P

AXES = ("grp", "blk")
N_Z = 8
N_BLK = 16
N_DEV = 256
LOG2E = math.log2(math.e)
LN2 = math.log(2.0)
VMEM_LIMIT = 48 * 1024 * 1024
TILE = 256
HALF = 80


def route(move):
    pairs = []
    for src in range(N_DEV):
        grp, blk = divmod(src, N_BLK)
        x_lo, z = divmod(grp, N_Z)
        x_lo, z, blk = move(x_lo, z, blk)
        pairs.append((src, (x_lo % 2 * N_Z + z % N_Z) * N_BLK + blk % N_BLK))
    return pairs


def send(array, move):
    return lax.ppermute(array, AXES, route(move))


def along_z(distance):
    return lambda x_lo, z, blk: (x_lo, z + distance, blk)


def along_blk(distance):
    return lambda x_lo, z, blk: (x_lo, z, blk + distance)


def other_core(x_lo, z, blk):
    return (x_lo, z, blk ^ 1)


def other_x(x_lo, z, blk):
    return (1 - x_lo, z, blk)


def outward(x_lo, z, blk):
    return (x_lo, z, blk + 4 if blk % 2 else blk - 4)


def homeward(x_lo, z, blk):
    return (x_lo, z, blk - 4 if blk % 2 else blk + 4)


def pair_body(n_chunks, n_sets, rows, scal_ref, base_ref, *refs):
    sets, refs = refs[:n_sets], refs[n_sets:]
    chunks, refs = refs[:n_chunks], refs[n_chunks:]
    grad_ref, cited_refs, loss_ref = refs[0], refs[1 : n_chunks + 1], refs[n_chunks + 1]
    cited_s, ids_s, part_s = refs[n_chunks + 2 :]
    slot = chunks[0].shape[0] // 5
    wide = 4 * slot
    cols = wide * n_chunks
    scale2, offset2, factor = scal_ref[0], scal_ref[1], scal_ref[2]
    member = lax.broadcasted_iota(jnp.int32, (slot, 128), 0)
    for kind in range(2):
        for n in range(n_chunks):
            for place, s in enumerate((0, 1, 2, 3 + kind)):
                at = pl.ds(n * wide + place * slot, slot)
                cited_s[kind, at] = chunks[n][s * slot : (s + 1) * slot]
                ids_s[kind, at] = (member + base_ref[n * 5 + s]).astype(jnp.float32)
    for q in range(n_sets):
        kind = q % 2
        ids = jnp.concatenate([ids_s[kind]] * (TILE // 128), axis=1)
        for t in range(rows // TILE):
            at = slice(t * TILE, (t + 1) * TILE)
            citing = sets[q][at]
            dots = lax.dot_general(
                cited_s[kind], citing, (((1,), (1,)), ((), ())), preferred_element_type=jnp.float32
            )
            target = sets[q][rows : rows + 16, at].astype(jnp.float32)
            target = target[0:1] * 256.0 + target[1:2]
            label = ids == target
            logit2 = dots * scale2 + offset2
            minus = -logit2
            small = jnp.exp2(jnp.minimum(logit2, minus))
            above = 1.0 + small
            sigmoid = jnp.where(logit2 >= 0, 1.0, small) * pl.reciprocal(above)
            grad = ((sigmoid - jnp.where(label, 1.0, 0.0)) * factor).astype(jnp.bfloat16)
            grad_ref[q, :, at] = grad
            linear = jnp.maximum(jnp.where(label, minus, logit2), 0.0)
            linear = jnp.sum(linear.reshape(cols // 8, 8, TILE), axis=0)
            prod = small[0:8]
            for k in range(8, cols, 8):
                prod = prod * above[k : k + 8] + small[k : k + 8]
            up = 1.0 + prod
            exact = up == 1.0
            log_part = jnp.where(
                exact, prod, jnp.log(up) * (prod / jnp.where(exact, 1.0, up - 1.0))
            )
            loss_ref[q : q + 1, at] = jnp.sum(linear * LN2 + log_part, axis=0, keepdims=True)
            part = jnp.dot(grad, citing, preferred_element_type=jnp.float32)
            if q < 2 and t == 0:
                part_s[kind] = part
            else:
                part_s[kind] += part
    for n in range(n_chunks):
        o = n * wide
        shared, last = slice(o, o + 3 * slot), slice(o + 3 * slot, o + wide)
        cited_refs[n][0 : 3 * slot] = (part_s[0, shared] + part_s[1, shared]).astype(jnp.bfloat16)
        cited_refs[n][3 * slot : wide] = part_s[0, last].astype(jnp.bfloat16)
        cited_refs[n][wide : wide + slot] = part_s[1, last].astype(jnp.bfloat16)


def pair_terms(scal, base, sets, chunks):
    n_sets, n_chunks = len(sets), len(chunks)
    rows, width = sets[0].shape[0] - 16, sets[0].shape[1]
    cols = chunks[0].shape[0] // 5 * 4 * n_chunks
    vmem = pl.BlockSpec(memory_space=pltpu.VMEM)
    smem = pl.BlockSpec(memory_space=pltpu.SMEM)
    out = pl.pallas_call(
        functools.partial(pair_body, n_chunks, n_sets, rows),
        out_shape=[jax.ShapeDtypeStruct((n_sets, cols, rows), jnp.bfloat16)]
        + [jax.ShapeDtypeStruct(c.shape, jnp.bfloat16) for c in chunks]
        + [jax.ShapeDtypeStruct((n_sets, rows), jnp.float32)],
        in_specs=[smem, smem] + [vmem] * (n_sets + n_chunks),
        out_specs=[vmem] * (n_chunks + 2),
        scratch_shapes=[
            pltpu.VMEM((2, cols, width), jnp.bfloat16),
            pltpu.VMEM((2, cols, 128), jnp.float32),
            pltpu.VMEM((2, cols, width), jnp.float32),
        ],
        compiler_params=pltpu.CompilerParams(vmem_limit_bytes=VMEM_LIMIT),
        cost_estimate=pl.CostEstimate(
            flops=8 * n_sets * rows * cols * width, bytes_accessed=8 * 2**20, transcendentals=0
        ),
        name="pair_terms",
    )(scal, base, *sets, *chunks)
    return out[0], out[1:-1], out[-1]


def citing_body(n_groups, n_chunks, kind, *refs):
    grads, refs = refs[:n_groups], refs[n_groups:]
    chunks, out_ref, cited_s = refs[:-2], refs[-2], refs[-1]
    slot = chunks[0].shape[0] // 5
    wide = 4 * slot
    for n, chunk in enumerate(chunks):
        for place, s in enumerate((0, 1, 2, 3 + kind)):
            at = pl.ds(n * wide + place * slot, slot)
            cited_s[at] = chunk[s * slot : (s + 1) * slot]
    cols = wide * n_chunks
    total = None
    for i in range(n_groups):
        term = lax.dot_general(
            grads[i][...],
            cited_s[i * cols : (i + 1) * cols],
            (((0,), (0,)), ((), ())),
            preferred_element_type=jnp.float32,
        )
        total = term if total is None else total + term
    out_ref[...] = total.astype(out_ref.dtype)


def citing_terms(grads, chunks, q, dtype):
    n_groups = len(grads)
    n_chunks = len(chunks) // n_groups
    _, cols, rows = grads[0].shape
    held, width = chunks[0].shape
    return pl.pallas_call(
        functools.partial(citing_body, n_groups, n_chunks, q % 2),
        grid=(1,),
        out_shape=jax.ShapeDtypeStruct((rows, width), dtype),
        in_specs=[pl.BlockSpec((None, cols, rows), lambda i: (q, 0, 0))] * n_groups
        + [pl.BlockSpec((held, width), lambda i: (0, 0))] * len(chunks),
        out_specs=pl.BlockSpec((rows, width), lambda i: (0, 0)),
        scratch_shapes=[pltpu.VMEM((cols * n_groups, width), jnp.bfloat16)],
        compiler_params=pltpu.CompilerParams(vmem_limit_bytes=VMEM_LIMIT),
        cost_estimate=pl.CostEstimate(
            flops=4 * rows * cols * n_groups * width, bytes_accessed=5 * 2**20, transcendentals=0
        ),
        name="citing_terms",
    )(*grads, *chunks)


def shards(source_vectors, reference_vectors, linked_target, score_multiplier, score_offset):
    f32, bf16 = jnp.float32, jnp.bfloat16
    rows, width = source_vectors.shape
    slot = reference_vectors.shape[0]
    blk = lax.axis_index("blk")
    grp = lax.axis_index("grp")
    x_lo, z = grp // N_Z, grp % N_Z
    averaging = 1.0 / math.sqrt(N_Z * 2 * N_BLK // 2 * slot)
    scal = jnp.stack(
        [
            score_multiplier[0] * LOG2E,
            score_offset[0] * LOG2E,
            score_multiplier[0] * averaging,
        ]
    )

    own = reference_vectors.astype(bf16)
    held = jnp.concatenate(
        [
            send(own, along_blk(2)),
            own,
            send(own, along_blk(-2)),
            send(own, along_blk(-4)),
            send(own, outward),
        ]
    )
    hi = (linked_target // 256).astype(bf16)
    lo = (linked_target % 256).astype(bf16)
    ids = jnp.concatenate([hi[None], lo[None], jnp.zeros((14, rows), bf16)])
    here = jnp.concatenate([source_vectors.astype(bf16), ids])
    here_other = send(here, other_core)
    there = send(here, other_x)
    there_other = send(there, other_core)
    sets = [here, here_other, there, there_other]

    chunk = {0: held}
    for sign in (1, -1):
        chunk[sign] = send(held, along_z(-sign))
        chunk[2 * sign] = send(held, along_z(-2 * sign))
    for sign in (1, -1):
        chunk[3 * sign] = send(chunk[2 * sign], along_z(-sign))
    chunk[4] = jnp.concatenate(
        [send(chunk[2][:HALF], along_z(-2)), send(chunk[-2][HALF:], along_z(2))]
    )

    slots = jnp.stack(
        [blk - 2, blk, blk + 2, blk + 4, jnp.where(blk % 2 == 1, blk - 4, blk + 4)]
    )
    slots = slots % N_BLK * slot

    def base_of(distance):
        return (x_lo * N_Z + (z + distance) % N_Z) * (N_BLK * slot) + slots

    groups = [(1, -1), (2, -2), (3, -3), (0, 4)]
    grads, part, losses = [], {}, []
    for group in groups:
        base = jnp.concatenate([base_of(d) for d in group]).astype(jnp.int32)
        grad, cited_part, loss = pair_terms(scal, base, sets, [chunk[d] for d in group])
        grads.append(grad)
        losses.append(loss)
        for d, term in zip(group, cited_part):
            part[d] = term

    chunks = [chunk[d] for group in groups for d in group]
    from_core = send(citing_terms(grads, chunks, 3, bf16), other_core)
    for_pair = citing_terms(grads, chunks, 2, f32) + from_core.astype(f32)
    from_pair = send(for_pair.astype(bf16), other_x)
    from_core = send(citing_terms(grads, chunks, 1, bf16), other_core)
    citing_grad = citing_terms(grads, chunks, 0, f32) + from_core.astype(f32)
    citing_grad = citing_grad + from_pair.astype(f32)

    loss = losses[0] + losses[1] + losses[2] + losses[3]
    from_core = send(jnp.stack([loss[1], loss[3]]), other_core)
    from_pair = send((loss[2] + from_core[1])[None], other_x)
    row_loss = (loss[0] + from_core[0] + from_pair[0]) * averaging

    on = send(part[3], along_z(1)).astype(f32) + part[2].astype(f32)
    on4 = send(part[4][:HALF], along_z(2)).astype(f32)
    back = send(part[-3], along_z(-1)).astype(f32) + part[-2].astype(f32)
    back4 = send(part[4][HALF:], along_z(-2)).astype(f32)
    on = jnp.concatenate([on[:HALF] + on4, on[HALF:]]).astype(bf16)
    back = jnp.concatenate([back[:HALF], back[HALF:] + back4]).astype(bf16)
    total = part[0].astype(f32)
    total = total + send(part[1], along_z(1)).astype(f32)
    total = total + send(part[-1], along_z(-1)).astype(f32)
    total = total + send(on, along_z(2)).astype(f32)
    total = total + send(back, along_z(-2)).astype(f32)
    back_home = total.astype(bf16)
    cited_grad = total[slot : 2 * slot]
    for s, move in (
        (0, along_blk(-2)),
        (2, along_blk(2)),
        (3, along_blk(4)),
        (4, homeward),
    ):
        cited_grad = cited_grad + send(back_home[s * slot : (s + 1) * slot], move).astype(f32)
    return (row_loss, citing_grad, cited_grad)


def solution(mesh):
    return jax.shard_map(
        shards,
        mesh=mesh,
        in_specs=(P(("grp", "blk"), None), P(("grp", "blk"), None), P(("grp", "blk")), P(), P()),
        out_specs=(P(("grp", "blk")), P(("grp", "blk"), None), P(("grp", "blk"), None)),
        check_vma=False,
    )
```

```python
import functools
import math

import jax
import jax.numpy as jnp
from jax import lax
from jax.experimental import pallas as pl
from jax.experimental.pallas import tpu as pltpu
from jax.sharding import PartitionSpec as P

AXES = ("grp", "blk")
N_Z = 8
N_BLK = 16
N_DEV = 256
LOG2E = math.log2(math.e)
LN2 = math.log(2.0)
VMEM_LIMIT = 48 * 1024 * 1024
TILE = 256


def route(move):
    pairs = []
    for src in range(N_DEV):
        grp, blk = divmod(src, N_BLK)
        x_lo, z = divmod(grp, N_Z)
        x_lo, z, blk = move(x_lo, z, blk)
        pairs.append((src, (x_lo % 2 * N_Z + z % N_Z) * N_BLK + blk % N_BLK))
    return pairs


def send(array, move):
    return lax.ppermute(array, AXES, route(move))


def along_z(distance):
    return lambda x_lo, z, blk: (x_lo, z + distance, blk)


def along_blk(distance):
    return lambda x_lo, z, blk: (x_lo, z, blk + distance)


def halfway(distance):
    return lambda x_lo, z, blk: (x_lo, z + (-distance if z % 2 else distance), blk)


def other_core(x_lo, z, blk):
    return (x_lo, z, blk ^ 1)


def other_x(x_lo, z, blk):
    return (1 - x_lo, z, blk)


def outward(x_lo, z, blk):
    return (x_lo, z, blk + 4 if blk % 2 else blk - 4)


def homeward(x_lo, z, blk):
    return (x_lo, z, blk - 4 if blk % 2 else blk + 4)


def pair_body(n_chunks, n_sets, rows, carried, with_loss, scal_ref, base_ref, *refs):
    sets, refs = refs[:n_sets], refs[n_sets:]
    chunks, refs = refs[:n_chunks], refs[n_chunks:]
    before, refs = refs[:carried], refs[carried:]
    loss_in, refs = refs[:with_loss], refs[with_loss:]
    grad_ref, cited_refs, loss_ref = refs[0], refs[1 : n_chunks + 1], refs[n_chunks + 1]
    cited_s, ids_s, part_s = refs[n_chunks + 2 :]
    slot = chunks[0].shape[0] // 5
    wide = 4 * slot
    cols = wide * n_chunks
    scale2, offset2, factor = scal_ref[0], scal_ref[1], scal_ref[2]
    member = lax.broadcasted_iota(jnp.int32, (slot, 128), 0)
    for kind in range(2):
        for n in range(n_chunks):
            for place, s in enumerate((0, 1, 2, 3 + kind)):
                at = pl.ds(n * wide + place * slot, slot)
                cited_s[kind, at] = chunks[n][s * slot : (s + 1) * slot]
                ids_s[kind, at] = (member + base_ref[n * 5 + s]).astype(jnp.float32)
    for q in range(n_sets):
        kind = q % 2
        ids = jnp.concatenate([ids_s[kind]] * (TILE // 128), axis=1)
        for t in range(rows // TILE):
            at = slice(t * TILE, (t + 1) * TILE)
            citing = sets[q][at]
            dots = lax.dot_general(
                cited_s[kind], citing, (((1,), (1,)), ((), ())), preferred_element_type=jnp.float32
            )
            target = sets[q][rows : rows + 16, at].astype(jnp.float32)
            target = target[0:1] * 256.0 + target[1:2]
            label = ids == target
            logit2 = dots * scale2 + offset2
            minus = -logit2
            small = jnp.exp2(jnp.minimum(logit2, minus))
            above = 1.0 + small
            sigmoid = jnp.where(logit2 >= 0, 1.0, small) * pl.reciprocal(above)
            grad = ((sigmoid - jnp.where(label, 1.0, 0.0)) * factor).astype(jnp.bfloat16)
            grad_ref[q, :, at] = grad
            linear = jnp.maximum(jnp.where(label, minus, logit2), 0.0)
            linear = jnp.sum(linear.reshape(cols // 8, 8, TILE), axis=0)
            prod = small[0:8]
            for k in range(8, cols, 8):
                prod = prod * above[k : k + 8] + small[k : k + 8]
            up = 1.0 + prod
            exact = up == 1.0
            log_part = jnp.where(
                exact, prod, jnp.log(up) * (prod / jnp.where(exact, 1.0, up - 1.0))
            )
            loss = jnp.sum(linear * LN2 + log_part, axis=0, keepdims=True)
            if with_loss:
                loss = loss + loss_in[0][q : q + 1, at]
            loss_ref[q : q + 1, at] = loss
            part = jnp.dot(grad, citing, preferred_element_type=jnp.float32)
            if q < 2 and t == 0:
                part_s[kind] = part
            else:
                part_s[kind] += part
    for n in range(n_chunks):
        o = n * wide
        shared, last = slice(o, o + 3 * slot), slice(o + 3 * slot, o + wide)
        pieces = (
            (slice(0, 3 * slot), part_s[0, shared] + part_s[1, shared]),
            (slice(3 * slot, wide), part_s[0, last]),
            (slice(wide, wide + slot), part_s[1, last]),
        )
        for at, piece in pieces:
            if carried:
                piece = piece + before[n][at]
            cited_refs[n][at] = piece.astype(cited_refs[n].dtype)


def pair_terms(scal, base, sets, chunks, before=(), loss=()):
    n_sets, n_chunks = len(sets), len(chunks)
    rows, width = sets[0].shape[0] - 16, sets[0].shape[1]
    cols = chunks[0].shape[0] // 5 * 4 * n_chunks
    vmem = pl.BlockSpec(memory_space=pltpu.VMEM)
    smem = pl.BlockSpec(memory_space=pltpu.SMEM)
    out = pl.pallas_call(
        functools.partial(pair_body, n_chunks, n_sets, rows, len(before), len(loss)),
        out_shape=[jax.ShapeDtypeStruct((n_sets, cols, rows), jnp.bfloat16)]
        + [jax.ShapeDtypeStruct(c.shape, jnp.bfloat16 if before else jnp.float32) for c in chunks]
        + [jax.ShapeDtypeStruct((n_sets, rows), jnp.float32)],
        in_specs=[smem, smem] + [vmem] * (n_sets + n_chunks + len(before) + len(loss)),
        out_specs=[vmem] * (n_chunks + 2),
        scratch_shapes=[
            pltpu.VMEM((2, cols, width), jnp.bfloat16),
            pltpu.VMEM((2, cols, 128), jnp.float32),
            pltpu.VMEM((2, cols, width), jnp.float32),
        ],
        compiler_params=pltpu.CompilerParams(vmem_limit_bytes=VMEM_LIMIT),
        cost_estimate=pl.CostEstimate(
            flops=n_sets * rows * cols * width, bytes_accessed=2**16, transcendentals=0
        ),
        name="pair_terms",
    )(scal, base, *sets, *chunks, *before, *loss)
    return out[0], out[1:-1], out[-1]


def citing_body(n_groups, n_chunks, kind, n_parts, final, *refs):
    grads, refs = refs[:n_groups], refs[n_groups:]
    chunks, refs = refs[: n_groups * n_chunks], refs[n_groups * n_chunks :]
    loss_ref, parts, refs = refs[0], refs[1 : n_parts + 1], refs[n_parts + 1 :]
    out_ref, cited_s = refs[0], refs[-1]
    slot = chunks[0].shape[0] // 5
    wide = 4 * slot
    for n, chunk in enumerate(chunks):
        for place, s in enumerate((0, 1, 2, 3 + kind)):
            at = pl.ds(n * wide + place * slot, slot)
            cited_s[at] = chunk[s * slot : (s + 1) * slot]
    cols = wide * n_chunks
    rows = grads[0].shape[1]
    total = None
    for i in range(n_groups):
        term = lax.dot_general(
            grads[i][...],
            cited_s[i * cols : (i + 1) * cols],
            (((0,), (0,)), ((), ())),
            preferred_element_type=jnp.float32,
        )
        total = term if total is None else total + term
    loss = loss_ref[kind : kind + 1]
    for part in parts:
        total = total + part[0:rows].astype(jnp.float32)
        tail = part[rows : rows + 16].astype(jnp.float32)
        loss = loss + (tail[0:1] + tail[1:2] + tail[2:3])
    if final:
        out_ref[...] = total
        refs[1][...] = loss * final
    else:
        out_ref[0:rows] = total.astype(jnp.bfloat16)
        high = loss.astype(jnp.bfloat16)
        rest = loss - high.astype(jnp.float32)
        middle = rest.astype(jnp.bfloat16)
        low = rest - middle.astype(jnp.float32)
        place = lax.broadcasted_iota(jnp.int32, (16, loss.shape[1]), 0)
        tail = jnp.where(place == 0, high.astype(jnp.float32), 0.0)
        tail = jnp.where(place == 1, middle.astype(jnp.float32), tail)
        tail = jnp.where(place == 2, low, tail)
        out_ref[rows : rows + 16] = tail.astype(jnp.bfloat16)


def citing_terms(grads, chunks, kind, loss, parts=(), final=0.0, weight=1):
    n_groups = len(grads)
    n_chunks = len(chunks) // n_groups
    _, cols, rows = grads[0].shape
    held, width = chunks[0].shape

    def whole(shape):
        return pl.BlockSpec(shape, lambda i: (0,) * len(shape))

    if final:
        out = [(rows, width), (1, rows)]
        out_shape = [jax.ShapeDtypeStruct(shape, jnp.float32) for shape in out]
    else:
        out = [(rows + 16, width)]
        out_shape = [jax.ShapeDtypeStruct(out[0], jnp.bfloat16)]
    got = pl.pallas_call(
        functools.partial(citing_body, n_groups, n_chunks, kind, len(parts), final),
        grid=(1,),
        out_shape=out_shape,
        in_specs=[pl.BlockSpec((None, cols, rows), lambda i: (kind, 0, 0))] * n_groups
        + [whole((held, width))] * len(chunks)
        + [whole(loss.shape)]
        + [whole((rows + 16, width))] * len(parts),
        out_specs=[whole(shape) for shape in out],
        scratch_shapes=[pltpu.VMEM((cols * n_groups, width), jnp.bfloat16)],
        compiler_params=pltpu.CompilerParams(vmem_limit_bytes=VMEM_LIMIT),
        cost_estimate=pl.CostEstimate(
            flops=weight * rows * cols * n_groups * width // 8, bytes_accessed=2**16, transcendentals=0
        ),
        name="citing_terms",
    )(*grads, *chunks, loss, *parts)
    return got if final else got[0]


def shards(source_vectors, reference_vectors, linked_target, score_multiplier, score_offset):
    f32, bf16 = jnp.float32, jnp.bfloat16
    rows, width = source_vectors.shape
    slot = reference_vectors.shape[0]
    blk = lax.axis_index("blk")
    grp = lax.axis_index("grp")
    x_lo, z = grp // N_Z, grp % N_Z
    averaging = 1.0 / math.sqrt(N_Z * 2 * N_BLK // 2 * slot)
    scal = jnp.stack(
        [
            score_multiplier[0] * LOG2E,
            score_offset[0] * LOG2E,
            score_multiplier[0] * averaging,
        ]
    )

    own = reference_vectors.astype(bf16)
    held = jnp.concatenate(
        [
            send(own, along_blk(2)),
            own,
            send(own, along_blk(-2)),
            send(own, along_blk(-4)),
            send(own, outward),
        ]
    )
    hi = (linked_target // 256).astype(bf16)
    lo = (linked_target % 256).astype(bf16)
    ids = jnp.concatenate([hi[None], lo[None], jnp.zeros((14, rows), bf16)])
    here = jnp.concatenate([source_vectors.astype(bf16), ids])
    here_other = send(here, other_core)
    held, outgoing, here_other = lax.optimization_barrier((held, here, here_other))
    there = send(outgoing, other_x)

    chunk = {0: held}
    for sign in (1, -1):
        chunk[2 * sign] = send(held, along_z(-2 * sign))
    for sign in (1, -1):
        chunk[sign] = send(held, along_z(-sign))
    near = lax.optimization_barrier(tuple(chunk[d] for d in (1, -1, 2, -2)))
    chunk.update(zip((1, -1, 2, -2), near))
    for sign in (1, -1):
        chunk[3 * sign] = send(chunk[2 * sign], along_z(-sign))
    even = z % 2 == 0
    chunk[4] = send(jnp.where(even, chunk[2], chunk[-2]), halfway(-2))
    slots = jnp.stack(
        [blk - 2, blk, blk + 2, blk + 4, jnp.where(blk % 2 == 1, blk - 4, blk + 4)]
    )
    slots = slots % N_BLK * slot

    def base_of(distance):
        return (x_lo * N_Z + (z + distance) % N_Z) * (N_BLK * slot) + slots

    groups = [(1, -1, 2, -2), (3, -3, 4, 0)]
    bases = [jnp.concatenate([base_of(d) for d in group]).astype(jnp.int32) for group in groups]
    chunks = [[chunk[d] for d in group] for group in groups]
    near_sets = [here, here_other]
    own_0 = pair_terms(scal, bases[0], near_sets, chunks[0])
    far = (chunk[3], chunk[-3], chunk[4], there, own_0[2])
    *far, there, own_0_loss = lax.optimization_barrier(far)
    chunks[1][:3] = far
    far_sets = [there, send(there, other_core)]
    own_1 = pair_terms(scal, bases[1], near_sets, chunks[1], loss=[own_0_loss])
    pair_1 = pair_terms(scal, bases[1], far_sets, chunks[1], own_1[1])
    pair_0 = pair_terms(scal, bases[0], far_sets, chunks[0], own_0[1], [pair_1[2]])
    part = dict(zip(groups[0] + groups[1], pair_0[1] + pair_1[1]))
    own_grads, pair_grads = [own_0[0], own_1[0]], [pair_0[0], pair_1[0]]
    own_loss, pair_loss = own_1[2], pair_0[2]
    chunks = chunks[0] + chunks[1]

    on = send(part[3], along_z(1))
    back = send(part[-3], along_z(-1))
    across = send(part[4], halfway(2))
    on, back, across, pair_loss = lax.optimization_barrier((on, back, across, pair_loss))

    from_core = send(citing_terms(pair_grads, chunks, 1, pair_loss), other_core)
    across = across.astype(f32)
    on = on.astype(f32) + part[2].astype(f32) + jnp.where(even, across, 0.0)
    back = back.astype(f32) + part[-2].astype(f32) + jnp.where(even, 0.0, across)
    on, back = on.astype(bf16), back.astype(bf16)
    on, back, part[1], part[-1] = lax.optimization_barrier((on, back, part[1], part[-1]))
    on = send(on, along_z(2))
    back = send(back, along_z(-2))
    for_pair = citing_terms(pair_grads, chunks, 0, pair_loss, [from_core])
    for_pair, own_loss = lax.optimization_barrier((for_pair, own_loss))
    from_pair = send(for_pair, other_x)
    from_core = send(citing_terms(own_grads, chunks, 1, own_loss, weight=160), other_core)
    citing_grad, row_loss = citing_terms(
        own_grads, chunks, 0, own_loss, [from_core, from_pair], averaging
    )

    total = part[0].astype(f32)
    total = total + send(part[1], along_z(1)).astype(f32)
    total = total + send(part[-1], along_z(-1)).astype(f32)
    total = total + on.astype(f32) + back.astype(f32)
    back_home = total.astype(bf16)
    home = []
    for s, move in (
        (3, along_blk(4)),
        (4, homeward),
        (0, along_blk(-2)),
        (2, along_blk(2)),
    ):
        home.append(send(back_home[s * slot : (s + 1) * slot], move))
    *home, row_loss = lax.optimization_barrier((*home, row_loss))
    cited_grad = total[slot : 2 * slot]
    for term in home:
        cited_grad = cited_grad + term.astype(f32)
    return (row_loss[0], citing_grad, cited_grad)


def solution(mesh):
    return jax.shard_map(
        shards,
        mesh=mesh,
        in_specs=(P(("grp", "blk"), None), P(("grp", "blk"), None), P(("grp", "blk")), P(), P()),
        out_specs=(P(("grp", "blk")), P(("grp", "blk"), None), P(("grp", "blk"), None)),
        check_vma=False,
    )
```

```python
import functools
import math

import jax
import jax.numpy as jnp
from jax import lax
from jax.experimental import pallas as pl
from jax.experimental.pallas import tpu as pltpu
from jax.sharding import PartitionSpec as P

AXES = ("grp", "blk")
N_Z = 8
N_BLK = 16
N_DEV = 256
LOG2E = math.log2(math.e)
LN2 = math.log(2.0)
VMEM_LIMIT = 20 * 1024 * 1024
TILE = 256
STRIP = 64


def route(move):
    pairs = []
    for src in range(N_DEV):
        grp, blk = divmod(src, N_BLK)
        x_lo, z = divmod(grp, N_Z)
        x_lo, z, blk = move(x_lo, z, blk)
        pairs.append((src, (x_lo % 2 * N_Z + z % N_Z) * N_BLK + blk % N_BLK))
    return pairs


def send(array, move):
    return lax.ppermute(array, AXES, route(move))


def along_z(distance):
    return lambda x_lo, z, blk: (x_lo, z + distance, blk)


def along_blk(distance):
    return lambda x_lo, z, blk: (x_lo, z, blk + distance)


def halfway(distance):
    return lambda x_lo, z, blk: (x_lo, z + (-distance if z % 2 else distance), blk)


def other_core(x_lo, z, blk):
    return (x_lo, z, blk ^ 1)


def other_z(x_lo, z, blk):
    return (x_lo, z ^ 1, blk)


def other_x(x_lo, z, blk):
    return (1 - x_lo, z, blk)


def outward(x_lo, z, blk):
    return (x_lo, z, blk + 4 if blk % 2 else blk - 4)


def homeward(x_lo, z, blk):
    return (x_lo, z, blk - 4 if blk % 2 else blk + 4)


def pair_body(n_chunks, n_sets, rows, carried, with_loss, scal_ref, base_ref, *refs):
    sets, refs = refs[:n_sets], refs[n_sets:]
    chunks, refs = refs[:n_chunks], refs[n_chunks:]
    before, refs = refs[:carried], refs[carried:]
    loss_in, refs = refs[:with_loss], refs[with_loss:]
    grad_ref, cited_refs, loss_ref = refs[0], refs[1 : n_chunks + 1], refs[n_chunks + 1]
    cited_s, ids_s, part_s = refs[n_chunks + 2 :]
    slot = chunks[0].shape[0] // 5
    wide = 4 * slot
    cols = wide * n_chunks
    scale2, offset2, factor = scal_ref[0], scal_ref[1], scal_ref[2]
    member = lax.broadcasted_iota(jnp.int32, (slot, 128), 0)
    for kind in range(2):
        for n in range(n_chunks):
            for place, s in enumerate((0, 1, 2, 3 + kind)):
                at = pl.ds(n * wide + place * slot, slot)
                cited_s[kind, at] = chunks[n][s * slot : (s + 1) * slot]
                ids_s[kind, at] = (member + base_ref[n * 5 + s]).astype(jnp.float32)
    steps = [(q, t) for q in range(n_sets) for t in range(rows // TILE)]

    def dots_of(step):
        q, t = step
        citing = sets[q][t * TILE : (t + 1) * TILE]
        return lax.dot_general(
            cited_s[q % 2], citing, (((1,), (1,)), ((), ())), preferred_element_type=jnp.float32
        )

    def finish(q):
        part_s[q % 2] = jnp.dot(
            grad_ref[q], sets[q][0:rows], preferred_element_type=jnp.float32
        )

    ahead = dots_of(steps[0])
    for i, (q, t) in enumerate(steps):
        kind = q % 2
        dots = ahead
        if i + 1 < len(steps):
            ahead = dots_of(steps[i + 1])
        at = slice(t * TILE, (t + 1) * TILE)
        target = sets[q][rows : rows + 16, at].astype(jnp.float32)
        target = target[0:1] * 256.0 + target[1:2]
        linear, prod = None, None
        for o in range(0, cols, STRIP):
            ids = jnp.concatenate([ids_s[kind, o : o + STRIP]] * (TILE // 128), axis=1)
            label = ids == target
            logit2 = dots[o : o + STRIP] * scale2 + offset2
            minus = -logit2
            small = jnp.exp2(jnp.minimum(logit2, minus))
            above = 1.0 + small
            sigmoid = jnp.where(logit2 >= 0, 1.0, small) * pl.reciprocal(above)
            grad = ((sigmoid - jnp.where(label, 1.0, 0.0)) * factor).astype(jnp.bfloat16)
            grad_ref[q, o : o + STRIP, at] = grad
            term = jnp.maximum(jnp.where(label, minus, logit2), 0.0)
            term = jnp.sum(term.reshape(STRIP // 8, 8, TILE), axis=0)
            linear = term if linear is None else linear + term
            for k in range(0, STRIP, 8):
                if prod is None:
                    prod = small[0:8]
                else:
                    prod = prod * above[k : k + 8] + small[k : k + 8]
        up = 1.0 + prod
        exact = up == 1.0
        log_part = jnp.where(
            exact, prod, jnp.log(up) * (prod / jnp.where(exact, 1.0, up - 1.0))
        )
        loss = jnp.sum(linear * LN2 + log_part, axis=0, keepdims=True)
        if with_loss:
            loss = loss + loss_in[0][q : q + 1, at]
        loss_ref[q : q + 1, at] = loss
        if t == rows // TILE - 1:
            finish(q)
    for n in range(n_chunks):
        o = n * wide
        shared, last = slice(o, o + 3 * slot), slice(o + 3 * slot, o + wide)
        pieces = (
            (slice(0, 3 * slot), part_s[0, shared] + part_s[1, shared]),
            (slice(3 * slot, wide), part_s[0, last]),
            (slice(wide, wide + slot), part_s[1, last]),
        )
        for at, piece in pieces:
            if carried:
                piece = piece + before[n][at]
            cited_refs[n][at] = piece.astype(cited_refs[n].dtype)


def pair_terms(scal, base, sets, chunks, before=(), loss=()):
    n_sets, n_chunks = len(sets), len(chunks)
    rows, width = sets[0].shape[0] - 16, sets[0].shape[1]
    cols = chunks[0].shape[0] // 5 * 4 * n_chunks
    vmem = pl.BlockSpec(memory_space=pltpu.VMEM)
    smem = pl.BlockSpec(memory_space=pltpu.SMEM)
    out = pl.pallas_call(
        functools.partial(pair_body, n_chunks, n_sets, rows, len(before), len(loss)),
        out_shape=[jax.ShapeDtypeStruct((n_sets, cols, rows), jnp.bfloat16)]
        + [jax.ShapeDtypeStruct(c.shape, jnp.bfloat16 if before else jnp.float32) for c in chunks]
        + [jax.ShapeDtypeStruct((n_sets, rows), jnp.float32)],
        in_specs=[smem, smem] + [vmem] * (n_sets + n_chunks + len(before) + len(loss)),
        out_specs=[vmem] * (n_chunks + 2),
        scratch_shapes=[
            pltpu.VMEM((2, cols, width), jnp.bfloat16),
            pltpu.VMEM((2, cols, 128), jnp.float32),
            pltpu.VMEM((2, cols, width), jnp.float32),
        ],
        compiler_params=pltpu.CompilerParams(vmem_limit_bytes=VMEM_LIMIT),
        cost_estimate=pl.CostEstimate(
            flops=n_sets * rows * cols * width, bytes_accessed=2**16, transcendentals=0
        ),
        name="pair_terms",
    )(scal, base, *sets, *chunks, *before, *loss)
    return out[0], out[1:-1], out[-1]


def kernel_params(flops):
    return dict(
        compiler_params=pltpu.CompilerParams(vmem_limit_bytes=VMEM_LIMIT),
        cost_estimate=pl.CostEstimate(flops=flops, bytes_accessed=2**16, transcendentals=0),
    )


def pack_loss(loss):
    high = loss.astype(jnp.bfloat16)
    rest = loss - high.astype(jnp.float32)
    middle = rest.astype(jnp.bfloat16)
    low = rest - middle.astype(jnp.float32)
    place = lax.broadcasted_iota(jnp.int32, (16, loss.shape[1]), 0)
    tail = jnp.where(place == 0, high.astype(jnp.float32), 0.0)
    tail = jnp.where(place == 1, middle.astype(jnp.float32), tail)
    tail = jnp.where(place == 2, low, tail)
    return tail.astype(jnp.bfloat16)


def unpack_loss(tail):
    tail = tail.astype(jnp.float32)
    return tail[0:1] + tail[1:2] + tail[2:3]


def citing_body(n_groups, n_sets, kind, *refs):
    grads, refs = refs[: n_sets * n_groups], refs[n_sets * n_groups :]
    losses, refs = refs[: n_sets * kind], refs[n_sets * kind :]
    chunks, out_ref, cited_s = refs[:-2], refs[-2], refs[-1]
    slot = chunks[0].shape[0] // 5
    wide = 4 * slot
    for n, chunk in enumerate(chunks):
        for place, s in enumerate((0, 1, 2, 3 + kind)):
            at = pl.ds(n * wide + place * slot, slot)
            cited_s[at] = chunk[s * slot : (s + 1) * slot]
    _, cols, rows = grads[0].shape
    for q in range(n_sets):
        total = None
        for i in range(n_groups):
            term = lax.dot_general(
                grads[q * n_groups + i][kind],
                cited_s[i * cols : (i + 1) * cols],
                (((0,), (0,)), ((), ())),
                preferred_element_type=jnp.float32,
            )
            total = term if total is None else total + term
        o = q * (rows + 16)
        out_ref[o : o + rows] = total.astype(out_ref.dtype)
        if kind:
            out_ref[o + rows : o + rows + 16] = pack_loss(losses[q][kind : kind + 1])


def citing_terms(grads, chunks, kind, losses):
    n_groups, n_sets = len(grads[0]), len(grads)
    _, cols, rows = grads[0][0].shape
    width = chunks[0].shape[1]
    vmem = pl.BlockSpec(memory_space=pltpu.VMEM)
    grads = [g for group in grads for g in group]
    losses = losses if kind else []
    shape = (n_sets * (rows + 16), width) if kind else (rows, width)
    return pl.pallas_call(
        functools.partial(citing_body, n_groups, n_sets, kind),
        out_shape=jax.ShapeDtypeStruct(shape, jnp.bfloat16 if kind else jnp.float32),
        in_specs=[vmem] * (len(grads) + len(losses) + len(chunks)),
        out_specs=vmem,
        scratch_shapes=[pltpu.VMEM((cols * n_groups, width), jnp.bfloat16)],
        name="citing_terms",
        **kernel_params(2**27),
    )(*grads, *losses, *chunks)


def message_body(term_ref, loss_ref, core_ref, out_ref):
    rows = term_ref.shape[0]
    total = term_ref[...] + core_ref[0:rows].astype(jnp.float32)
    out_ref[0:rows] = total.astype(jnp.bfloat16)
    loss = loss_ref[0:1] + unpack_loss(core_ref[rows : rows + 16])
    out_ref[rows : rows + 16] = pack_loss(loss)


def message(term, loss, from_core):
    rows, width = term.shape
    vmem = pl.BlockSpec(memory_space=pltpu.VMEM)
    return pl.pallas_call(
        message_body,
        out_shape=jax.ShapeDtypeStruct((rows + 16, width), jnp.bfloat16),
        in_specs=[vmem] * 3,
        out_specs=vmem,
        name="message",
        **kernel_params(2**20),
    )(term, loss, from_core)


def final_body(averaging, term_ref, loss_ref, core_ref, pair_ref, out_ref, row_loss_ref):
    rows = term_ref.shape[0]
    o = rows + 16
    total = term_ref[...] + core_ref[o : o + rows].astype(jnp.float32)
    out_ref[...] = total + pair_ref[0:rows].astype(jnp.float32)
    loss = loss_ref[0:1] + unpack_loss(core_ref[o + rows : o + rows + 16])
    row_loss_ref[...] = (loss + unpack_loss(pair_ref[rows : rows + 16])) * averaging


def final_terms(term, loss, from_core, from_pair, averaging):
    rows, width = term.shape
    vmem = pl.BlockSpec(memory_space=pltpu.VMEM)
    return pl.pallas_call(
        functools.partial(final_body, averaging),
        out_shape=[
            jax.ShapeDtypeStruct((rows, width), jnp.float32),
            jax.ShapeDtypeStruct((1, rows), jnp.float32),
        ],
        in_specs=[vmem] * 4,
        out_specs=[vmem] * 2,
        name="final_terms",
        **kernel_params(2**20),
    )(term, loss, from_core, from_pair)


def shards(source_vectors, reference_vectors, linked_target, score_multiplier, score_offset):
    f32, bf16 = jnp.float32, jnp.bfloat16
    rows, width = source_vectors.shape
    slot = reference_vectors.shape[0]
    blk = lax.axis_index("blk")
    grp = lax.axis_index("grp")
    x_lo, z = grp // N_Z, grp % N_Z
    averaging = 1.0 / math.sqrt(N_Z * 2 * N_BLK // 2 * slot)
    scal = jnp.stack(
        [
            score_multiplier[0] * LOG2E,
            score_offset[0] * LOG2E,
            score_multiplier[0] * averaging,
        ]
    )

    own = reference_vectors.astype(bf16)
    held = jnp.concatenate(
        [
            send(own, along_blk(2)),
            own,
            send(own, along_blk(-2)),
            send(own, along_blk(-4)),
            send(own, outward),
        ]
    )
    hi = (linked_target // 256).astype(bf16)
    lo = (linked_target % 256).astype(bf16)
    ids = jnp.concatenate([hi[None], lo[None], jnp.zeros((14, rows), bf16)])
    here = jnp.concatenate([source_vectors.astype(bf16), ids])
    cut = (rows + 32) // 32 * 16
    held, first, second = lax.optimization_barrier((held, here[:cut], here[cut:]))
    first = send(first, other_x)
    second = send(second, other_x)

    chunk = {0: held}
    for step in (1, 2):
        for sign in (1, -1):
            chunk[step * sign] = send(chunk[(step - 1) * sign], along_z(-sign))
    near = (chunk[2], chunk[-2], here, first)
    chunk[2], chunk[-2], swapped, first = lax.optimization_barrier(near)
    here_other = send(swapped, other_core)
    for sign in (1, -1):
        chunk[3 * sign] = send(chunk[2 * sign], along_z(-sign))
    even = z % 2 == 0
    chunk[4] = send(jnp.where(even, chunk[-3], chunk[3]), other_z)

    slots = jnp.stack(
        [blk - 2, blk, blk + 2, blk + 4, jnp.where(blk % 2 == 1, blk - 4, blk + 4)]
    )
    slots = slots % N_BLK * slot

    def base_of(distance):
        return (x_lo * N_Z + (z + distance) % N_Z) * (N_BLK * slot) + slots

    groups = [(1, -1, 2, -2), (3, -3, 4, 0)]
    bases = [jnp.concatenate([base_of(d) for d in group]).astype(jnp.int32) for group in groups]
    chunks = [[chunk[d] for d in group] for group in groups]
    near_sets = [here, here_other]
    own_0 = pair_terms(scal, bases[0], near_sets, chunks[0])
    far = (chunk[3], chunk[-3], chunk[4], own_0[2], first, second)
    *far, own_0_loss, first, second = lax.optimization_barrier(far)
    there = jnp.concatenate([first, second])
    chunks[1][:3] = far
    far_sets = [there, send(there, other_core)]
    own_1 = pair_terms(scal, bases[1], near_sets, chunks[1], loss=[own_0_loss])
    pair_1 = pair_terms(scal, bases[1], far_sets, chunks[1], own_1[1])
    pair_0 = pair_terms(scal, bases[0], far_sets, chunks[0], own_0[1], [pair_1[2]])
    part = dict(zip(groups[0] + groups[1], pair_0[1] + pair_1[1]))
    own_grads, pair_grads = [own_0[0], own_1[0]], [pair_0[0], pair_1[0]]
    own_loss, pair_loss = own_1[2], pair_0[2]
    chunks = chunks[0] + chunks[1]

    on = send(part[3], along_z(1))
    back = send(part[-3], along_z(-1))
    across = send(part[4], halfway(2))

    for_core = citing_terms([pair_grads, own_grads], chunks, 1, [pair_loss, own_loss])
    on, back, across, for_core = lax.optimization_barrier((on, back, across, for_core))
    from_core = send(for_core, other_core)
    across = across.astype(f32)
    on = on.astype(f32) + part[2].astype(f32) + jnp.where(even, across, 0.0)
    back = back.astype(f32) + part[-2].astype(f32) + jnp.where(even, 0.0, across)
    on, back = on.astype(bf16), back.astype(bf16)
    on, back, part[1], part[-1] = lax.optimization_barrier((on, back, part[1], part[-1]))
    on = send(on, along_z(2))
    back = send(back, along_z(-2))
    for_pair = message(citing_terms([pair_grads], chunks, 0, []), pair_loss, from_core)
    from_pair = send(for_pair, other_x)
    for_pair, own_loss, own_grads[0] = lax.optimization_barrier(
        (for_pair, own_loss, own_grads[0])
    )
    citing_grad = citing_terms([own_grads], chunks, 0, [])

    total = part[0].astype(f32)
    total = total + send(part[1], along_z(1)).astype(f32)
    total = total + send(part[-1], along_z(-1)).astype(f32)
    total = total + on.astype(f32) + back.astype(f32)
    back_home = total.astype(bf16)
    citing_grad, row_loss = final_terms(
        citing_grad, own_loss, from_core, from_pair, averaging
    )
    home = []
    for s, move in (
        (3, along_blk(4)),
        (4, homeward),
        (0, along_blk(-2)),
        (2, along_blk(2)),
    ):
        home.append(send(back_home[s * slot : (s + 1) * slot], move))
    *home, row_loss = lax.optimization_barrier((*home, row_loss[0]))
    cited_grad = total[slot : 2 * slot]
    for term in home:
        cited_grad = cited_grad + term.astype(f32)
    return (row_loss, citing_grad, cited_grad)


def solution(mesh):
    return jax.shard_map(
        shards,
        mesh=mesh,
        in_specs=(P(("grp", "blk"), None), P(("grp", "blk"), None), P(("grp", "blk")), P(), P()),
        out_specs=(P(("grp", "blk")), P(("grp", "blk"), None), P(("grp", "blk"), None)),
        check_vma=False,
    )
```

```python
import functools
import math

import jax
import jax.numpy as jnp
from jax import lax
from jax.experimental import pallas as pl
from jax.experimental.pallas import tpu as pltpu
from jax.sharding import PartitionSpec as P

AXES = ("grp", "blk")
N_Z = 8
N_BLK = 16
N_DEV = 256
LOG2E = math.log2(math.e)
LN2 = math.log(2.0)
VMEM_LIMIT = 20 * 1024 * 1024
TILE = 256
STRIP = 64


def route(move):
    pairs = []
    for src in range(N_DEV):
        grp, blk = divmod(src, N_BLK)
        x_lo, z = divmod(grp, N_Z)
        x_lo, z, blk = move(x_lo, z, blk)
        pairs.append((src, (x_lo % 2 * N_Z + z % N_Z) * N_BLK + blk % N_BLK))
    return pairs


def send(array, move):
    return lax.ppermute(array, AXES, route(move))


def along_z(distance):
    return lambda x_lo, z, blk: (x_lo, z + distance, blk)


def along_blk(distance):
    return lambda x_lo, z, blk: (x_lo, z, blk + distance)


def halfway(distance):
    return lambda x_lo, z, blk: (x_lo, z + (-distance if z % 2 else distance), blk)


def other_core(x_lo, z, blk):
    return (x_lo, z, blk ^ 1)


def other_z(x_lo, z, blk):
    return (x_lo, z ^ 1, blk)


def other_x(x_lo, z, blk):
    return (1 - x_lo, z, blk)


def outward(x_lo, z, blk):
    return (x_lo, z, blk + 4 if blk % 2 else blk - 4)


def homeward(x_lo, z, blk):
    return (x_lo, z, blk - 4 if blk % 2 else blk + 4)


def pair_body(n_chunks, n_sets, rows, carried, with_loss, scal_ref, base_ref, *refs):
    sets, refs = refs[:n_sets], refs[n_sets:]
    chunks, refs = refs[:n_chunks], refs[n_chunks:]
    before, refs = refs[:carried], refs[carried:]
    loss_in, refs = refs[:with_loss], refs[with_loss:]
    grad_ref, cited_refs, loss_ref = refs[0], refs[1 : n_chunks + 1], refs[n_chunks + 1]
    cited_s, ids_s, part_s = refs[n_chunks + 2 :]
    slot = chunks[0].shape[0] // 5
    wide = 4 * slot
    cols = wide * n_chunks
    scale2, offset2, factor = scal_ref[0], scal_ref[1], scal_ref[2]
    member = lax.broadcasted_iota(jnp.int32, (slot, 128), 0)
    for kind in range(2):
        for n in range(n_chunks):
            for place, s in enumerate((0, 1, 2, 3 + kind)):
                at = pl.ds(n * wide + place * slot, slot)
                cited_s[kind, at] = chunks[n][s * slot : (s + 1) * slot]
                ids_s[kind, at] = (member + base_ref[n * 5 + s]).astype(jnp.float32)
    steps = [(q, t) for q in range(n_sets) for t in range(rows // TILE)]

    def dots_of(step):
        q, t = step
        citing = sets[q][t * TILE : (t + 1) * TILE]
        return lax.dot_general(
            cited_s[q % 2], citing, (((1,), (1,)), ((), ())), preferred_element_type=jnp.float32
        )

    def finish(q):
        part_s[q % 2] = jnp.dot(
            grad_ref[q], sets[q][0:rows], preferred_element_type=jnp.float32
        )

    ahead = dots_of(steps[0])
    for i, (q, t) in enumerate(steps):
        kind = q % 2
        dots = ahead
        if i + 1 < len(steps):
            ahead = dots_of(steps[i + 1])
        at = slice(t * TILE, (t + 1) * TILE)
        target = sets[q][rows : rows + 16, at].astype(jnp.float32)
        target = target[0:1] * 256.0 + target[1:2]
        linear, prod = None, None
        for o in range(0, cols, STRIP):
            ids = jnp.concatenate([ids_s[kind, o : o + STRIP]] * (TILE // 128), axis=1)
            label = ids == target
            logit2 = dots[o : o + STRIP] * scale2 + offset2
            minus = -logit2
            small = jnp.exp2(jnp.minimum(logit2, minus))
            above = 1.0 + small
            sigmoid = jnp.where(logit2 >= 0, 1.0, small) * pl.reciprocal(above)
            grad = ((sigmoid - jnp.where(label, 1.0, 0.0)) * factor).astype(jnp.bfloat16)
            grad_ref[q, o : o + STRIP, at] = grad
            term = jnp.maximum(jnp.where(label, minus, logit2), 0.0)
            term = jnp.sum(term.reshape(STRIP // 8, 8, TILE), axis=0)
            linear = term if linear is None else linear + term
            for k in range(0, STRIP, 8):
                if prod is None:
                    prod = small[0:8]
                else:
                    prod = prod * above[k : k + 8] + small[k : k + 8]
        up = 1.0 + prod
        exact = up == 1.0
        log_part = jnp.where(
            exact, prod, jnp.log(up) * (prod / jnp.where(exact, 1.0, up - 1.0))
        )
        loss = jnp.sum(linear * LN2 + log_part, axis=0, keepdims=True)
        if with_loss:
            loss = loss + loss_in[0][q : q + 1, at]
        loss_ref[q : q + 1, at] = loss
        if t == rows // TILE - 1:
            finish(q)
    for n in range(n_chunks):
        o = n * wide
        shared, last = slice(o, o + 3 * slot), slice(o + 3 * slot, o + wide)
        pieces = (
            (slice(0, 3 * slot), part_s[0, shared] + part_s[1, shared]),
            (slice(3 * slot, wide), part_s[0, last]),
            (slice(wide, wide + slot), part_s[1, last]),
        )
        for at, piece in pieces:
            if carried:
                piece = piece + before[n][at]
            cited_refs[n][at] = piece.astype(cited_refs[n].dtype)


def pair_terms(scal, base, sets, chunks, before=(), loss=()):
    n_sets, n_chunks = len(sets), len(chunks)
    rows, width = sets[0].shape[0] - 16, sets[0].shape[1]
    cols = chunks[0].shape[0] // 5 * 4 * n_chunks
    vmem = pl.BlockSpec(memory_space=pltpu.VMEM)
    smem = pl.BlockSpec(memory_space=pltpu.SMEM)
    out = pl.pallas_call(
        functools.partial(pair_body, n_chunks, n_sets, rows, len(before), len(loss)),
        out_shape=[jax.ShapeDtypeStruct((n_sets, cols, rows), jnp.bfloat16)]
        + [jax.ShapeDtypeStruct(c.shape, jnp.bfloat16 if before else jnp.float32) for c in chunks]
        + [jax.ShapeDtypeStruct((n_sets, rows), jnp.float32)],
        in_specs=[smem, smem] + [vmem] * (n_sets + n_chunks + len(before) + len(loss)),
        out_specs=[vmem] * (n_chunks + 2),
        scratch_shapes=[
            pltpu.VMEM((2, cols, width), jnp.bfloat16),
            pltpu.VMEM((2, cols, 128), jnp.float32),
            pltpu.VMEM((2, cols, width), jnp.float32),
        ],
        compiler_params=pltpu.CompilerParams(vmem_limit_bytes=VMEM_LIMIT),
        cost_estimate=pl.CostEstimate(
            flops=n_sets * rows * cols * width, bytes_accessed=2**16, transcendentals=0
        ),
        name="pair_terms",
    )(scal, base, *sets, *chunks, *before, *loss)
    return out[0], out[1:-1], out[-1]


def kernel_params(flops):
    return dict(
        compiler_params=pltpu.CompilerParams(vmem_limit_bytes=VMEM_LIMIT),
        cost_estimate=pl.CostEstimate(flops=flops, bytes_accessed=2**16, transcendentals=0),
    )


def pack_loss(loss):
    high = loss.astype(jnp.bfloat16)
    rest = loss - high.astype(jnp.float32)
    middle = rest.astype(jnp.bfloat16)
    low = rest - middle.astype(jnp.float32)
    place = lax.broadcasted_iota(jnp.int32, (16, loss.shape[1]), 0)
    tail = jnp.where(place == 0, high.astype(jnp.float32), 0.0)
    tail = jnp.where(place == 1, middle.astype(jnp.float32), tail)
    tail = jnp.where(place == 2, low, tail)
    return tail.astype(jnp.bfloat16)


def unpack_loss(tail):
    tail = tail.astype(jnp.float32)
    return tail[0:1] + tail[1:2] + tail[2:3]


def citing_body(n_groups, n_sets, kind, *refs):
    grads, refs = refs[: n_sets * n_groups], refs[n_sets * n_groups :]
    losses, refs = refs[: n_sets * kind], refs[n_sets * kind :]
    chunks, out_ref, cited_s = refs[:-2], refs[-2], refs[-1]
    slot = chunks[0].shape[0] // 5
    wide = 4 * slot
    for n, chunk in enumerate(chunks):
        for place, s in enumerate((0, 1, 2, 3 + kind)):
            at = pl.ds(n * wide + place * slot, slot)
            cited_s[at] = chunk[s * slot : (s + 1) * slot]
    _, cols, rows = grads[0].shape
    for q in range(n_sets):
        total = None
        for i in range(n_groups):
            term = lax.dot_general(
                grads[q * n_groups + i][kind],
                cited_s[i * cols : (i + 1) * cols],
                (((0,), (0,)), ((), ())),
                preferred_element_type=jnp.float32,
            )
            total = term if total is None else total + term
        o = q * (rows + 16)
        out_ref[o : o + rows] = total.astype(out_ref.dtype)
        if kind:
            out_ref[o + rows : o + rows + 16] = pack_loss(losses[q][kind : kind + 1])


def citing_terms(grads, chunks, kind, losses):
    n_groups, n_sets = len(grads[0]), len(grads)
    _, cols, rows = grads[0][0].shape
    width = chunks[0].shape[1]
    vmem = pl.BlockSpec(memory_space=pltpu.VMEM)
    grads = [g for group in grads for g in group]
    losses = losses if kind else []
    shape = (n_sets * (rows + 16), width) if kind else (rows, width)
    return pl.pallas_call(
        functools.partial(citing_body, n_groups, n_sets, kind),
        out_shape=jax.ShapeDtypeStruct(shape, jnp.bfloat16 if kind else jnp.float32),
        in_specs=[vmem] * (len(grads) + len(losses) + len(chunks)),
        out_specs=vmem,
        scratch_shapes=[pltpu.VMEM((cols * n_groups, width), jnp.bfloat16)],
        name="citing_terms",
        **kernel_params(2**27),
    )(*grads, *losses, *chunks)


def message_body(term_ref, loss_ref, core_ref, out_ref):
    rows = term_ref.shape[0]
    total = term_ref[...] + core_ref[0:rows].astype(jnp.float32)
    out_ref[0:rows] = total.astype(jnp.bfloat16)
    loss = loss_ref[0:1] + unpack_loss(core_ref[rows : rows + 16])
    out_ref[rows : rows + 16] = pack_loss(loss)


def message(term, loss, from_core):
    rows, width = term.shape
    vmem = pl.BlockSpec(memory_space=pltpu.VMEM)
    return pl.pallas_call(
        message_body,
        out_shape=jax.ShapeDtypeStruct((rows + 16, width), jnp.bfloat16),
        in_specs=[vmem] * 3,
        out_specs=vmem,
        name="message",
        **kernel_params(2**20),
    )(term, loss, from_core)


def final_body(averaging, term_ref, loss_ref, core_ref, pair_ref, out_ref, row_loss_ref):
    rows = term_ref.shape[0]
    o = rows + 16
    total = term_ref[...] + core_ref[o : o + rows].astype(jnp.float32)
    out_ref[...] = total + pair_ref[0:rows].astype(jnp.float32)
    loss = loss_ref[0:1] + unpack_loss(core_ref[o + rows : o + rows + 16])
    row_loss_ref[...] = (loss + unpack_loss(pair_ref[rows : rows + 16])) * averaging


def final_terms(term, loss, from_core, from_pair, averaging):
    rows, width = term.shape
    vmem = pl.BlockSpec(memory_space=pltpu.VMEM)
    return pl.pallas_call(
        functools.partial(final_body, averaging),
        out_shape=[
            jax.ShapeDtypeStruct((rows, width), jnp.float32),
            jax.ShapeDtypeStruct((1, rows), jnp.float32),
        ],
        in_specs=[vmem] * 4,
        out_specs=[vmem] * 2,
        name="final_terms",
        **kernel_params(2**20),
    )(term, loss, from_core, from_pair)


def shards(source_vectors, reference_vectors, linked_target, score_multiplier, score_offset):
    f32, bf16 = jnp.float32, jnp.bfloat16
    rows, width = source_vectors.shape
    slot = reference_vectors.shape[0]
    blk = lax.axis_index("blk")
    grp = lax.axis_index("grp")
    x_lo, z = grp // N_Z, grp % N_Z
    averaging = 1.0 / math.sqrt(N_Z * 2 * N_BLK // 2 * slot)
    scal = jnp.stack(
        [
            score_multiplier[0] * LOG2E,
            score_offset[0] * LOG2E,
            score_multiplier[0] * averaging,
        ]
    )

    own = reference_vectors.astype(bf16)
    held = jnp.concatenate(
        [
            send(own, along_blk(2)),
            own,
            send(own, along_blk(-2)),
            send(own, along_blk(-4)),
            send(own, outward),
        ]
    )
    hi = (linked_target // 256).astype(bf16)
    lo = (linked_target % 256).astype(bf16)
    ids = jnp.concatenate([hi[None], lo[None], jnp.zeros((14, rows), bf16)])
    here = jnp.concatenate([source_vectors.astype(bf16), ids])
    cut = (rows + 32) // 32 * 16
    held, first, second = lax.optimization_barrier((held, here[:cut], here[cut:]))
    first = send(first, other_x)
    second = send(second, other_x)

    chunk = {0: held}
    for step in (1, 2):
        for sign in (1, -1):
            chunk[step * sign] = send(chunk[(step - 1) * sign], along_z(-sign))
    near = (chunk[2], chunk[-2], here, first)
    chunk[2], chunk[-2], swapped, first = lax.optimization_barrier(near)
    here_other = send(swapped, other_core)
    for sign in (1, -1):
        chunk[3 * sign] = send(chunk[2 * sign], along_z(-sign))
    even = z % 2 == 0
    chunk[4] = send(jnp.where(even, chunk[-3], chunk[3]), other_z)

    slots = jnp.stack(
        [blk - 2, blk, blk + 2, blk + 4, jnp.where(blk % 2 == 1, blk - 4, blk + 4)]
    )
    slots = slots % N_BLK * slot

    def base_of(distance):
        return (x_lo * N_Z + (z + distance) % N_Z) * (N_BLK * slot) + slots

    groups = [(1, -1, 2, -2), (3, -3, 4, 0)]
    bases = [jnp.concatenate([base_of(d) for d in group]).astype(jnp.int32) for group in groups]
    chunks = [[chunk[d] for d in group] for group in groups]
    near_sets = [here, here_other]
    own_0 = pair_terms(scal, bases[0], near_sets, chunks[0])
    far = (chunk[3], chunk[-3], chunk[4], own_0[2], first, second)
    *far, own_0_loss, first, second = lax.optimization_barrier(far)
    there = jnp.concatenate([first, second])
    chunks[1][:3] = far
    far_sets = [there, send(there, other_core)]
    own_1 = pair_terms(scal, bases[1], near_sets, chunks[1], loss=[own_0_loss])
    pair_1 = pair_terms(scal, bases[1], far_sets, chunks[1], own_1[1])
    pair_0 = pair_terms(scal, bases[0], far_sets, chunks[0], own_0[1], [pair_1[2]])
    part = dict(zip(groups[0] + groups[1], pair_0[1] + pair_1[1]))
    own_grads, pair_grads = [own_0[0], own_1[0]], [pair_0[0], pair_1[0]]
    own_loss, pair_loss = own_1[2], pair_0[2]
    chunks = chunks[0] + chunks[1]

    on = send(part[3], along_z(1))
    back = send(part[-3], along_z(-1))
    across = send(part[4], halfway(2))

    for_core = citing_terms([pair_grads, own_grads], chunks, 1, [pair_loss, own_loss])
    on, back, across, for_core = lax.optimization_barrier((on, back, across, for_core))
    from_core = send(for_core, other_core)
    across = across.astype(f32)
    on = on.astype(f32) + part[2].astype(f32) + jnp.where(even, across, 0.0)
    back = back.astype(f32) + part[-2].astype(f32) + jnp.where(even, 0.0, across)
    on, back = on.astype(bf16), back.astype(bf16)
    on = send(on, along_z(1)).astype(f32) + part[1].astype(f32)
    back = send(back, along_z(-1)).astype(f32) + part[-1].astype(f32)
    on = send(on.astype(bf16), along_z(1))
    back = send(back.astype(bf16), along_z(-1))
    for_pair = message(citing_terms([pair_grads], chunks, 0, []), pair_loss, from_core)
    from_pair = send(for_pair, other_x)
    for_pair, own_loss, own_grads[0] = lax.optimization_barrier(
        (for_pair, own_loss, own_grads[0])
    )
    citing_grad = citing_terms([own_grads], chunks, 0, [])

    total = part[0].astype(f32)
    total = total + on.astype(f32) + back.astype(f32)
    back_home = total.astype(bf16)
    citing_grad, row_loss = final_terms(
        citing_grad, own_loss, from_core, from_pair, averaging
    )
    home = []
    for s, move in (
        (3, along_blk(4)),
        (4, homeward),
        (0, along_blk(-2)),
        (2, along_blk(2)),
    ):
        home.append(send(back_home[s * slot : (s + 1) * slot], move))
    *home, row_loss = lax.optimization_barrier((*home, row_loss[0]))
    cited_grad = total[slot : 2 * slot]
    for term in home:
        cited_grad = cited_grad + term.astype(f32)
    return (row_loss, citing_grad, cited_grad)


def solution(mesh):
    return jax.shard_map(
        shards,
        mesh=mesh,
        in_specs=(P(("grp", "blk"), None), P(("grp", "blk"), None), P(("grp", "blk")), P(), P()),
        out_specs=(P(("grp", "blk")), P(("grp", "blk"), None), P(("grp", "blk"), None)),
        check_vma=False,
    )
```
